256 devices in a mesh: section: 16 (over y, x), expert: 16 (over z, core).
Axes of the slice: x: 4, y: 4, z: 8, core: 2. Of those that a mesh axis runs over, the one named last changes fastest.
Arguments:
- acts: bfloat16 [2, 128, 2048], P(None, 'expert'), may hold values from -6 to 6
- norm_gain: float32 [16, 2048], P('section'), may hold values from 0.1 to 1.9
- gate_w: bfloat16 [16, 16, 2048, 768], P('section', 'expert'), may hold values from -0.125 to 0.125
- up_w: bfloat16 [16, 16, 2048, 768], P('section', 'expert'), may hold values from -0.125 to 0.125
- down_w: bfloat16 [16, 16, 768, 2048], P('section', 'expert'), may hold values from -0.21875 to 0.21875
- route_ids: int32 [16, 2, 128, 2], P('section', None, 'expert'), may hold values from 0 to 15, all different within a row; in each aligned block of 8 rows (0 to 7, 8 to 15, ..., all dimensions but the last counted through in order) at most 2 rows name the same one
- route_probs: float32 [16, 2, 128, 2], P('section', None, 'expert'), may hold values from 0.2 to 1
Outputs:
- layer_outputs: float32 [16, 2, 128, 2048], P('section', None, 'expert')
- hessians: float32 [16, 16, 768, 768], P('section', 'expert')
The draws below stay inside these ranges and needn't reach their ends.
Inputs may be any that keep to these rules, and one draw needn't show every extreme that they name: `route_ids`: each token names 2 different experts; in one layer and micro-batch the 8 tokens of one index of expert name one expert at most 2 times, a bound that some block reaches in some of these groups.
All inputs are finite; a program needn't handle non-finite values.
Results may differ from the reference program's by a relative error of at most 0.04.
Values may be sent and summed in bfloat16 or wider, within the bound.
No kernel may reach another device: no remote copies, remote signals or barrier semaphores. Data moves between devices by JAX's collectives and lax.ppermute only.
A program may use at most 64 MiB of HBM per device.

```python
import math
import jax
import jax.numpy as jnp
import numpy as np
from jax import lax

D = 2048
FFW = 768
TOPK = 2
TOK_DEV = 8
MB = 2
EXPERTS = 16
LAYERS = 16
TOKENS = 128
CAP = 2
N_EXPERT = 16


def block_levels(rng, shape, pieces, least, high):
    level, own = 1.0, jax.random.fold_in(rng, 6)
    for position, parts in pieces:
        draws = jnp.exp(jax.random.uniform(jax.random.fold_in(own, position), (parts,), jnp.float32, least / len(pieces), high / len(pieces)))
        level = level * jnp.repeat(draws, shape[position] // parts).reshape([-1 if axis == position else 1 for axis in range(len(shape))])
    return level


def routed_block(stream_key, own, number, rows, number_of, top, limit, slope):
    sequence = jax.random.permutation(stream_key, number_of)
    packed, usual = portions_of(number_of, rows * top, limit, slope, True), portions_of(number_of, rows * top, limit, slope, False)
    places = jnp.arange(number_of)

    def named(lengths, turn):
        used = int((lengths > 0).sum())
        fixed = max(1, used // 4)
        shifted = fixed + (places - fixed + turn * (used - fixed)) % max(1, number_of - fixed)
        return jnp.zeros((number_of,), jnp.int32).at[sequence[jnp.where(places < fixed, places, shifted)]].set(jnp.asarray(lengths, jnp.int32))

    lengths = jnp.where(number % 4 == 0, named(packed, number // 4), named(usual, number - number // 4 - 1))
    mixed = jax.random.permutation(jax.random.fold_in(own, 3), number_of)
    donor, taker = mixed[0:number_of // 2 * 2:2], mixed[1:number_of // 2 * 2:2]
    room = jnp.minimum(lengths[donor] - 1, limit - lengths[taker]) // 2
    room = jnp.where((donor == sequence[0]) | (taker == sequence[0]) | (lengths[taker] == 0), 0, jnp.maximum(room, 0))
    shifted = jax.random.randint(jax.random.fold_in(own, 4), (number_of // 2,), 0, 1 << 20) % (room + 1)
    lengths = lengths.at[donor].add(-shifted).at[taker].add(shifted)
    members = jnp.searchsorted(jnp.cumsum(lengths), jnp.arange(rows * top), side="right").astype(jnp.int32)
    listing = members.reshape(top, rows).T
    listing = listing[jax.random.permutation(jax.random.fold_in(own, 1), rows)]
    turn = jax.random.randint(jax.random.fold_in(own, 2), (rows, 1), 0, top)
    return jnp.take_along_axis(listing, (jnp.arange(top)[None, :] + turn) % top, axis=1)


def portions_of(number_of, total, limit, lean, full):
    weights = [(1 << 20) // math.isqrt(grade ** lean) + 1 for grade in range(1, number_of + 1)]
    largest = limit if full else min(limit, max(-(-total // number_of), total * weights[0] // sum(weights)))
    least = 1 if total - largest >= number_of - 1 else 0
    holding, spare = [largest] + [least] * (number_of - 1), total - largest - least * (number_of - 1)
    while spare > 0:
        free = [i for i in range(1, number_of) if holding[i] < largest] or [i for i in range(1, number_of) if holding[i] < limit]
        whole, left = sum([weights[i] for i in free]), spare
        for i in free:
            addition = min(limit - holding[i], max(1, left * weights[i] // whole), spare)
            holding[i] = holding[i] + addition
            spare = spare - addition
    return np.array(holding)


def scatter_about(key, dims, width, most, cuts=(), kind=jnp.bfloat16):
    values = width * jax.random.normal(key, dims, jnp.float32)
    if cuts:
        values = values * block_levels(key, dims, cuts, -0.22, 0.18)
    return jnp.clip(values, -most, most).astype(kind)


def setup_inputs(seed: int = 0) -> dict:
    splits = jax.random.split(jax.random.key(seed), 8)
    acts = scatter_about(splits[0], (MB, TOKENS, D), 1.0, 6.0, ((1, 16),))
    norm_gain = jnp.clip(1.0 + 0.18 * jax.random.normal(splits[1], (LAYERS, D), jnp.float32), 0.1, 1.9)
    gate_w = scatter_about(splits[2], (LAYERS, EXPERTS, D, FFW), D ** -0.5, 0.125, ((0, 16), (1, 16)))
    up_w = scatter_about(splits[3], (LAYERS, EXPERTS, D, FFW), D ** -0.5, 0.125, ((0, 16), (1, 16)))
    down_w = scatter_about(splits[4], (LAYERS, EXPERTS, FFW, D), FFW ** -0.5, 0.21875, ((0, 16), (1, 16)))
    route_ids_keys = jax.random.split(jax.random.fold_in(splits[5], 1), LAYERS * MB * TOKENS // TOK_DEV)
    route_ids_turns = jax.random.permutation(jax.random.fold_in(splits[5], 3), LAYERS * MB * TOKENS // TOK_DEV)
    route_ids = jax.vmap(lambda own, number: routed_block(jax.random.fold_in(splits[5], 2), own, number, TOK_DEV, EXPERTS, TOPK, CAP, 2))(route_ids_keys, route_ids_turns).reshape((LAYERS, MB, TOKENS, TOPK))
    route_probs = jnp.clip(0.2 + 0.8 * jax.random.uniform(splits[6], (LAYERS, MB, TOKENS, TOPK), jnp.float32) ** block_levels(splits[6], (LAYERS, MB, TOKENS, TOPK), ((0, 16), (2, 16)), -0.2, 0.2), 0.2, 1.0)
    return dict(acts=acts, norm_gain=norm_gain, gate_w=gate_w, up_w=up_w, down_w=down_w, route_ids=route_ids, route_probs=route_probs)


def reference(acts, norm_gain, gate_w, up_w, down_w, route_ids, route_probs):
    scale = 2.0 / (MB * TOK_DEV * TOPK)
    assigns = TOK_DEV * TOPK
    source = jnp.broadcast_to(jnp.arange(N_EXPERT, dtype=jnp.int32)[:, None], (N_EXPERT, assigns)).astype(jnp.int32)
    best = lax.Precision.HIGHEST
    current = acts.astype(jnp.float32)
    layer_list = []
    hess_list = []
    for layer in range(LAYERS):
        gate_full = gate_w[layer].astype(jnp.float32)
        up_full = up_w[layer].astype(jnp.float32)
        down_full = down_w[layer].astype(jnp.float32)
        outputs = []
        hessian = jnp.zeros((EXPERTS, FFW, FFW), jnp.float32)
        for batch in range(MB):
            wide = current[batch]
            normed = (wide * lax.rsqrt(lax.optimization_barrier(jnp.mean(wide * wide, axis=-1, keepdims=True)) + 1e-06) * norm_gain[layer]).astype(jnp.bfloat16)
            chosen = route_ids[layer, batch].reshape(N_EXPERT, assigns).astype(jnp.int32)
            onehot = (chosen[..., None] == jnp.arange(EXPERTS, dtype=jnp.int32)).astype(jnp.int32)
            slot = lax.optimization_barrier(jnp.sum((jnp.cumsum(onehot, axis=1) - onehot) * onehot, axis=-1)).astype(jnp.int32)
            spread = jnp.repeat(normed, TOPK, axis=0).reshape(N_EXPERT, assigns, D)
            buffer = jnp.zeros((EXPERTS, N_EXPERT, CAP, D), jnp.bfloat16).at[chosen, source, slot].set(spread)
            rows = buffer.reshape(EXPERTS, N_EXPERT * CAP, D).astype(jnp.float32)
            gate = jnp.einsum('erd,edf->erf', rows, gate_full, precision=best)
            upper = jnp.einsum('erd,edf->erf', rows, up_full, precision=best)
            hidden = (jax.nn.silu(gate) * upper).astype(jnp.bfloat16)
            hidden_full = hidden.astype(jnp.float32)
            output = jnp.einsum('erf,efd->erd', hidden_full, down_full, precision=best).astype(jnp.bfloat16)
            output = output.reshape(EXPERTS, N_EXPERT, CAP, D)
            picked = output[chosen, source, slot].astype(jnp.float32).reshape(TOKENS, TOPK, D)
            mixed = lax.optimization_barrier(jnp.sum(route_probs[layer, batch][..., None] * picked, axis=1))
            outputs.append(wide + mixed)
            hessian = hessian + jnp.einsum('erf,erg->efg', hidden_full, hidden_full, precision=best)
        current = jnp.stack(outputs)
        layer_list.append(current)
        hess_list.append(scale * hessian)
    return (jnp.stack(layer_list), jnp.stack(hess_list))
```

```python
import functools

import jax
import jax.numpy as jnp
from jax import lax
from jax.experimental import pallas as pl
from jax.experimental.pallas import tpu as pltpu
from jax.sharding import PartitionSpec as P

LANES = 128
SLOTS = 2
BF16 = jnp.bfloat16
F32 = jnp.float32


def vmem():
    return pl.BlockSpec(memory_space=pltpu.VMEM)


def smem():
    return pl.BlockSpec(memory_space=pltpu.SMEM)


def spread_rows(rows, spare, owners):
    blocks = rows.shape[1] // LANES
    for slot in range(SLOTS):
        for block in range(blocks):
            spare[pl.ds(slot * blocks + block, owners, stride=SLOTS * blocks), :] = rows[
                slot * owners : (slot + 1) * owners, block * LANES : (block + 1) * LANES
            ]


def gather_rows(spare, owners, blocks):
    parts = []
    for slot in range(SLOTS):
        parts.append(
            jnp.concatenate(
                [
                    spare[pl.ds(slot * blocks + block, owners, stride=SLOTS * blocks), :]
                    for block in range(blocks)
                ],
                axis=1,
            )
        )
    return jnp.concatenate(parts, axis=0)


def tables_kernel(owners, ids_ref, probs_ref, send_ref, take_ref):
    batches, tokens, picks = ids_ref.shape
    experts = lax.broadcasted_iota(jnp.int32, (tokens, owners), 1)
    earlier = (
        lax.broadcasted_iota(jnp.int32, (tokens, tokens), 0)
        > lax.broadcasted_iota(jnp.int32, (tokens, tokens), 1)
    ).astype(BF16)
    for batch in range(batches):
        ids = ids_ref[batch]
        probs = probs_ref[batch]
        named = jnp.zeros((tokens, owners), F32)
        weight = jnp.zeros((tokens, owners), F32)
        for pick in range(picks):
            hit = ids[:, pick : pick + 1] == experts
            named = named + jnp.where(hit, 1.0, 0.0)
            weight = weight + jnp.where(hit, probs[:, pick : pick + 1], 0.0)
        slot = jnp.dot(earlier, named.astype(BF16), preferred_element_type=F32)
        split = [jnp.abs(slot - number) < 0.5 for number in range(SLOTS)]
        send = jnp.concatenate([jnp.where(own, named, 0.0) for own in split], axis=1)
        take = jnp.concatenate([jnp.where(own, weight, 0.0) for own in split], axis=1)
        send_ref[batch] = send.astype(BF16)
        high = take.astype(BF16).astype(F32)
        take_ref[batch] = jnp.concatenate([high, take - high], axis=0).astype(BF16)


def dispatch_kernel(step, owners, held_ref, x_ref, gain_ref, send_ref, out_ref, spare):
    wide = x_ref[...].astype(F32)
    mean = jnp.mean(wide * wide, axis=-1, keepdims=True)
    normed = (wide * lax.rsqrt(mean + 1e-06) * gain_ref[...]).astype(BF16)
    rows = lax.dot_general(
        send_ref[held_ref[step]], normed, (((0,), (0,)), ((), ())), preferred_element_type=F32
    )
    spread_rows(rows, spare, owners)
    out_ref[...] = spare[...].astype(BF16).reshape(out_ref.shape)


def expert_kernel(in_ref, gate_ref, up_ref, down_ref, out_ref, hidden_ref, spare):
    owners, height, lanes = in_ref.shape
    spare[...] = in_ref[...].astype(F32).reshape(owners * height, lanes)
    rows = gather_rows(spare, owners, height // SLOTS).astype(BF16)
    gate = jnp.dot(rows, gate_ref[...], preferred_element_type=F32)
    upper = jnp.dot(rows, up_ref[...], preferred_element_type=F32)
    hidden = (gate / (1.0 + jnp.exp(-gate)) * upper).astype(BF16)
    hidden_ref[...] = hidden
    output = jnp.dot(hidden, down_ref[...], preferred_element_type=F32)
    spread_rows(output, spare, owners)
    out_ref[...] = spare[...].astype(BF16).reshape(out_ref.shape)


def combine_kernel(step, held_ref, x_ref, back_ref, take_ref, out_ref, sent_ref, spare):
    owners, height, lanes = back_ref.shape
    tokens = x_ref.shape[0]
    spare[...] = back_ref[...].astype(F32).reshape(owners * height, lanes)
    rows = gather_rows(spare, owners, height // SLOTS).astype(BF16)
    mixed = jnp.dot(take_ref[held_ref[step]], rows, preferred_element_type=F32)
    result = x_ref[...].astype(F32) + (mixed[:tokens] + mixed[tokens:])
    out_ref[...] = result
    sent_ref[...] = result.astype(BF16)


def body(acts, norm_gain, gate_w, up_w, down_w, route_ids, route_probs):
    sections = lax.axis_size("section")
    section = lax.axis_index("section")
    owners = lax.axis_size("expert")
    batches, tokens, feature = acts.shape
    picks = route_ids.shape[-1]
    hidden_width = gate_w.shape[-1]
    steps = batches + sections - 1
    height = SLOTS * feature // LANES
    scale = 2.0 / (batches * tokens * picks)
    w_gate, w_up, w_down = gate_w[0, 0], up_w[0, 0], down_w[0, 0]
    packed = jax.ShapeDtypeStruct((owners, height, LANES), BF16)
    spare = [pltpu.VMEM((owners * height, LANES), F32)]

    send, take = pl.pallas_call(
        functools.partial(tables_kernel, owners),
        out_shape=(
            jax.ShapeDtypeStruct((batches, tokens, SLOTS * owners), BF16),
            jax.ShapeDtypeStruct((batches, 2 * tokens, SLOTS * owners), BF16),
        ),
        in_specs=[vmem()] * 2,
        out_specs=(vmem(), vmem()),
        name="tables",
    )(route_ids[0], route_probs[0])
    held = jnp.clip(jnp.arange(steps, dtype=jnp.int32) - section, 0, batches - 1)

    layer_out = [jnp.zeros((tokens, feature), F32)] * batches
    hiddens = [jnp.zeros((SLOTS * owners, hidden_width), BF16)] * batches
    arrived = acts[0]
    for step in range(steps):
        if 0 < step < batches:
            arrived = jnp.where(section == 0, acts[step], arrived)
        outgoing = pl.pallas_call(
            functools.partial(dispatch_kernel, step, owners),
            out_shape=packed,
            in_specs=[smem()] + [vmem()] * 3,
            out_specs=vmem(),
            scratch_shapes=spare,
            name="dispatch",
        )(held, arrived, norm_gain, send)
        incoming = lax.all_to_all(outgoing, "expert", split_axis=0, concat_axis=0, tiled=True)
        output, hidden = pl.pallas_call(
            expert_kernel,
            out_shape=(packed, jax.ShapeDtypeStruct((SLOTS * owners, hidden_width), BF16)),
            in_specs=[vmem()] * 4,
            out_specs=(vmem(), vmem()),
            scratch_shapes=spare,
            name="expert",
        )(incoming, w_gate, w_up, w_down)
        back = lax.all_to_all(output, "expert", split_axis=0, concat_axis=0, tiled=True)
        result, sent = pl.pallas_call(
            functools.partial(combine_kernel, step),
            out_shape=(
                jax.ShapeDtypeStruct((tokens, feature), F32),
                jax.ShapeDtypeStruct((tokens, feature), BF16),
            ),
            in_specs=[smem()] + [vmem()] * 3,
            out_specs=(vmem(), vmem()),
            scratch_shapes=spare,
            name="combine",
        )(held, arrived, back, take)
        for batch in range(batches):
            own = step - section == batch
            layer_out[batch] = jnp.where(own, result, layer_out[batch])
            hiddens[batch] = jnp.where(own, hidden, hiddens[batch])
        if step < steps - 1:
            pairs = [
                (step - batch, step - batch + 1)
                for batch in range(batches)
                if 0 <= step - batch < sections - 1
            ]
            arrived = lax.ppermute(sent, "section", pairs)
    rows = jnp.concatenate(hiddens, axis=0)
    square = lax.dot_general(rows, rows, (((0,), (0,)), ((), ())), preferred_element_type=F32)
    return (jnp.stack(layer_out)[None], (scale * square)[None, None])


def solution(mesh):
    placed = (
        P(None, "expert", None),
        P("section", None),
        P("section", "expert", None, None),
        P("section", "expert", None, None),
        P("section", "expert", None, None),
        P("section", None, "expert", None),
        P("section", None, "expert", None),
    )
    return jax.shard_map(
        body,
        mesh=mesh,
        in_specs=placed,
        out_specs=(P("section", None, "expert", None), P("section", "expert", None, None)),
        check_vma=False,
    )
```

```python
import functools

import jax
import jax.numpy as jnp
from jax import lax
from jax.experimental import pallas as pl
from jax.experimental.pallas import tpu as pltpu
from jax.sharding import PartitionSpec as P

LANES = 128
SLOTS = 2
BF16 = jnp.bfloat16
F32 = jnp.float32


MIB = 1 << 20


def params(mib):
    return pltpu.CompilerParams(vmem_limit_bytes=mib * MIB)


def vmem():
    return pl.BlockSpec(memory_space=pltpu.VMEM)


def spread_rows(rows, spare, owners):
    blocks = rows.shape[1] // LANES
    for slot in range(SLOTS):
        for block in range(blocks):
            spare[pl.ds(slot * blocks + block, owners, stride=SLOTS * blocks), :] = rows[
                slot * owners : (slot + 1) * owners, block * LANES : (block + 1) * LANES
            ]


def gather_rows(spare, owners, blocks):
    parts = []
    for slot in range(SLOTS):
        parts.append(
            jnp.concatenate(
                [
                    spare[pl.ds(slot * blocks + block, owners, stride=SLOTS * blocks), :]
                    for block in range(blocks)
                ],
                axis=1,
            )
        )
    return jnp.concatenate(parts, axis=0)


def weights_kernel(*refs):
    hidden_ref = refs[-1]
    hidden_ref[...] = jnp.zeros_like(hidden_ref)


def tables_kernel(owners, ids_ref, probs_ref, send_ref, take_ref, layer_ref):
    layer_ref[...] = jnp.zeros_like(layer_ref)
    batches, picks, tokens = ids_ref.shape
    experts = lax.broadcasted_iota(jnp.int32, (owners, tokens), 0)
    earlier = (
        lax.broadcasted_iota(jnp.int32, (tokens, tokens), 0)
        < lax.broadcasted_iota(jnp.int32, (tokens, tokens), 1)
    ).astype(BF16)
    for batch in range(batches):
        ids = ids_ref[batch]
        probs = probs_ref[batch]
        named = jnp.zeros((owners, tokens), F32)
        weight = jnp.zeros((owners, tokens), F32)
        for pick in range(picks):
            hit = ids[pick : pick + 1, :] == experts
            named = named + jnp.where(hit, 1.0, 0.0)
            weight = weight + jnp.where(hit, probs[pick : pick + 1, :], 0.0)
        slot = jnp.dot(named.astype(BF16), earlier, preferred_element_type=F32)
        split = [jnp.abs(slot - number) < 0.5 for number in range(SLOTS)]
        send = jnp.concatenate([jnp.where(own, named, 0.0) for own in split], axis=0)
        take = jnp.concatenate([jnp.where(own, weight, 0.0) for own in split], axis=0)
        send_ref[batch] = send.astype(BF16)
        high = take.astype(BF16).astype(F32)
        take_ref[batch] = jnp.concatenate([high, take - high], axis=1).astype(BF16)


def when_active(step, batches):
    batch = step - lax.axis_index("section")

    def call(function):
        pl.when((batch >= 0) & (batch < batches))(lambda: function(batch))

    return call


def dispatch_kernel(step, owners, batches, *refs):
    *sources, gain_ref, send_ref, out_ref, x_ref, spare = refs

    @when_active(step, batches)
    def _(held):
        if step == 0:
            x = sources[0][0]
        elif step < batches:
            x = jnp.where(held == step, sources[1][step], sources[0][...])
        else:
            x = sources[0][...]
        x_ref[...] = x
        wide = x.astype(F32)
        mean = jnp.mean(wide * wide, axis=-1, keepdims=True)
        normed = (wide * lax.rsqrt(mean + 1e-06) * gain_ref[...]).astype(BF16)
        rows = jnp.dot(send_ref[held], normed, preferred_element_type=F32)
        spread_rows(rows, spare, owners)
        out_ref[...] = spare[...].astype(BF16).reshape(out_ref.shape)


def expert_kernel(step, batches, in_ref, gate_ref, up_ref, down_ref, _, out_ref, hidden_ref, spare):
    owners, height, lanes = in_ref.shape

    @when_active(step, batches)
    def _(held):
        spare[...] = in_ref[...].astype(F32).reshape(owners * height, lanes)
        rows = gather_rows(spare, owners, height // SLOTS).astype(BF16)
        gate = jnp.dot(rows, gate_ref[...], preferred_element_type=F32)
        upper = jnp.dot(rows, up_ref[...], preferred_element_type=F32)
        hidden = (gate / (1.0 + jnp.exp(-gate)) * upper).astype(BF16)
        hidden_ref[held] = hidden
        output = jnp.dot(hidden, down_ref[...], preferred_element_type=F32)
        spread_rows(output, spare, owners)
        out_ref[...] = spare[...].astype(BF16).reshape(out_ref.shape)


def combine_kernel(
    step, batches, last, x_ref, back_ref, take_ref, before_ref, sent_ref, out_ref, spare
):
    owners, height, lanes = back_ref.shape
    tokens = x_ref.shape[0]
    if last:
        out_ref[...] = before_ref[...]

    @when_active(step, batches)
    def _(held):
        spare[...] = back_ref[...].astype(F32).reshape(owners * height, lanes)
        rows = gather_rows(spare, owners, height // SLOTS).astype(BF16)
        mixed = lax.dot_general(
            take_ref[held], rows, (((0,), (0,)), ((), ())), preferred_element_type=F32
        )
        result = x_ref[...].astype(F32) + (mixed[:tokens] + mixed[tokens:])
        sent_ref[...] = result.astype(BF16)
        out_ref[held] = result


def onward(step, batches, sections):
    row = 4 if sections % 4 == 0 else sections
    needed = [step - batch for batch in range(batches) if 0 <= step - batch < sections - 1]
    if step % row < row - 2:
        return [(place, place + 1) for place in needed]
    if any((place + 1) % row == 0 for place in needed):
        row = sections
    return [(place, place - place % row + (place + 1) % row) for place in range(sections)]


def body(acts, norm_gain, gate_w, up_w, down_w, route_ids, route_probs):
    sections = lax.axis_size("section")
    owners = lax.axis_size("expert")
    batches, tokens, feature = acts.shape
    picks = route_ids.shape[-1]
    hidden_width = gate_w.shape[-1]
    steps = batches + sections - 1
    height = SLOTS * feature // LANES
    scale = 2.0 / (batches * tokens * picks)
    w_gate, w_up, w_down = gate_w[0, 0], up_w[0, 0], down_w[0, 0]
    packed = jax.ShapeDtypeStruct((owners, height, LANES), BF16)
    held_x = jax.ShapeDtypeStruct((tokens, feature), BF16)
    hidden_shape = jax.ShapeDtypeStruct((batches, SLOTS * owners, hidden_width), BF16)
    layer_shape = jax.ShapeDtypeStruct((batches, tokens, feature), F32)
    spare = [pltpu.VMEM((owners * height, LANES), F32)]

    hiddens = pl.pallas_call(
        weights_kernel,
        out_shape=hidden_shape,
        in_specs=[vmem()] * 3,
        out_specs=vmem(),
        compiler_params=params(2),
        cost_estimate=pl.CostEstimate(
            flops=0, bytes_accessed=4 * 3 * w_gate.size, transcendentals=0
        ),
        name="weights",
    )(w_gate, w_up, w_down)
    send, take, layer_out = pl.pallas_call(
        functools.partial(tables_kernel, owners),
        out_shape=(
            jax.ShapeDtypeStruct((batches, SLOTS * owners, tokens), BF16),
            jax.ShapeDtypeStruct((batches, SLOTS * owners, 2 * tokens), BF16),
            layer_shape,
        ),
        in_specs=[vmem()] * 2,
        out_specs=(vmem(),) * 3,
        compiler_params=params(2),
        name="tables",
    )(jnp.swapaxes(route_ids[0], 1, 2), jnp.swapaxes(route_probs[0], 1, 2))

    sources = [acts]
    for step in range(steps):
        last = step == steps - 1
        outgoing, wide = pl.pallas_call(
            functools.partial(dispatch_kernel, step, owners, batches),
            out_shape=(packed, held_x),
            in_specs=[vmem()] * (len(sources) + 2),
            out_specs=(vmem(), vmem()),
            scratch_shapes=spare,
            compiler_params=params(2),
            name="dispatch",
        )(*sources, norm_gain, send)
        incoming = lax.all_to_all(outgoing, "expert", split_axis=0, concat_axis=0, tiled=True)
        output, hiddens = pl.pallas_call(
            functools.partial(expert_kernel, step, batches),
            out_shape=(packed, hidden_shape),
            in_specs=[vmem()] * 5,
            out_specs=(vmem(), vmem()),
            scratch_shapes=spare,
            input_output_aliases={4: 1},
            compiler_params=params(2),
            name="expert",
        )(incoming, w_gate, w_up, w_down, hiddens)
        back = lax.all_to_all(output, "expert", split_axis=0, concat_axis=0, tiled=True)
        sent, layer_out = pl.pallas_call(
            functools.partial(combine_kernel, step, batches, last),
            out_shape=(held_x, layer_shape),
            in_specs=[vmem()] * 4,
            out_specs=(vmem(), vmem()),
            scratch_shapes=spare,
            input_output_aliases={} if last else {3: 1},
            compiler_params=params(2),
            name="combine",
        )(wide, back, take, layer_out)
        if not last:
            arrived = lax.ppermute(sent, "section", onward(step, batches, sections))
            sources = [arrived, acts] if step + 1 < batches else [arrived]
    rows = hiddens.reshape(batches * SLOTS * owners, hidden_width)
    square = lax.dot_general(rows, rows, (((0,), (0,)), ((), ())), preferred_element_type=F32)
    return (layer_out[None], (scale * square)[None, None])


def solution(mesh):
    placed = (
        P(None, "expert", None),
        P("section", None),
        P("section", "expert", None, None),
        P("section", "expert", None, None),
        P("section", "expert", None, None),
        P("section", None, "expert", None),
        P("section", None, "expert", None),
    )
    return jax.shard_map(
        body,
        mesh=mesh,
        in_specs=placed,
        out_specs=(P("section", None, "expert", None), P("section", "expert", None, None)),
        check_vma=False,
    )
```

```python
import functools

import jax
import jax.numpy as jnp
from jax import lax
from jax.experimental import pallas as pl
from jax.experimental.pallas import tpu as pltpu
from jax.sharding import PartitionSpec as P

LANES = 128
SLOTS = 2
BF16 = jnp.bfloat16
F32 = jnp.float32


MIB = 1 << 20


def params(mib):
    return pltpu.CompilerParams(vmem_limit_bytes=mib * MIB)


def vmem():
    return pl.BlockSpec(memory_space=pltpu.VMEM)


def spread_rows(rows, spare, owners):
    blocks = rows.shape[1] // LANES
    for slot in range(SLOTS):
        for block in range(blocks):
            spare[pl.ds(slot * blocks + block, owners, stride=SLOTS * blocks), :] = rows[
                slot * owners : (slot + 1) * owners, block * LANES : (block + 1) * LANES
            ]


def gather_rows(spare, owners, blocks):
    parts = []
    for slot in range(SLOTS):
        parts.append(
            jnp.concatenate(
                [
                    spare[pl.ds(slot * blocks + block, owners, stride=SLOTS * blocks), :]
                    for block in range(blocks)
                ],
                axis=1,
            )
        )
    return jnp.concatenate(parts, axis=0)


def weights_kernel(*refs):
    hidden_ref = refs[-1]
    hidden_ref[...] = jnp.zeros_like(hidden_ref)


def tables_kernel(owners, ids_ref, probs_ref, send_ref, take_ref, layer_ref):
    layer_ref[...] = jnp.zeros_like(layer_ref)
    batches, picks, tokens = ids_ref.shape
    experts = lax.broadcasted_iota(jnp.int32, (owners, tokens), 0)
    earlier = (
        lax.broadcasted_iota(jnp.int32, (tokens, tokens), 0)
        < lax.broadcasted_iota(jnp.int32, (tokens, tokens), 1)
    ).astype(BF16)
    for batch in range(batches):
        ids = ids_ref[batch]
        probs = probs_ref[batch]
        named = jnp.zeros((owners, tokens), F32)
        weight = jnp.zeros((owners, tokens), F32)
        for pick in range(picks):
            hit = ids[pick : pick + 1, :] == experts
            named = named + jnp.where(hit, 1.0, 0.0)
            weight = weight + jnp.where(hit, probs[pick : pick + 1, :], 0.0)
        slot = jnp.dot(named.astype(BF16), earlier, preferred_element_type=F32)
        split = [jnp.abs(slot - number) < 0.5 for number in range(SLOTS)]
        send = jnp.concatenate([jnp.where(own, named, 0.0) for own in split], axis=0)
        take = jnp.concatenate([jnp.where(own, weight, 0.0) for own in split], axis=0)
        send_ref[batch] = send.astype(BF16)
        high = take.astype(BF16).astype(F32)
        take_ref[batch] = jnp.concatenate([high, take - high], axis=1).astype(BF16)


def when_active(step, batches):
    batch = step - lax.axis_index("section")

    def call(function):
        pl.when((batch >= 0) & (batch < batches))(lambda: function(batch))

    return call


def dispatch_kernel(step, owners, batches, *refs):
    *sources, gain_ref, send_ref, out_ref, x_ref, spare = refs

    @when_active(step, batches)
    def _(held):
        if step == 0:
            x = sources[0][0]
        elif step < batches:
            x = jnp.where(held == step, sources[1][step], sources[0][...])
        else:
            x = sources[0][...]
        x_ref[...] = x
        wide = x.astype(F32)
        mean = jnp.mean(wide * wide, axis=-1, keepdims=True)
        normed = (wide * lax.rsqrt(mean + 1e-06) * gain_ref[...]).astype(BF16)
        rows = jnp.dot(send_ref[held], normed, preferred_element_type=F32)
        spread_rows(rows, spare, owners)
        out_ref[...] = spare[...].astype(BF16).reshape(out_ref.shape)


def expert_kernel(step, batches, in_ref, gate_ref, up_ref, down_ref, _, out_ref, hidden_ref, spare):
    owners, height, lanes = in_ref.shape

    @when_active(step, batches)
    def _(held):
        spare[...] = in_ref[...].astype(F32).reshape(owners * height, lanes)
        rows = gather_rows(spare, owners, height // SLOTS).astype(BF16)
        gate = jnp.dot(rows, gate_ref[...], preferred_element_type=F32)
        upper = jnp.dot(rows, up_ref[...], preferred_element_type=F32)
        hidden = (gate / (1.0 + jnp.exp(-gate)) * upper).astype(BF16)
        hidden_ref[held] = hidden
        output = jnp.dot(hidden, down_ref[...], preferred_element_type=F32)
        spread_rows(output, spare, owners)
        out_ref[...] = spare[...].astype(BF16).reshape(out_ref.shape)


def combine_kernel(
    step, batches, last, x_ref, back_ref, take_ref, before_ref, sent_ref, out_ref, spare
):
    owners, height, lanes = back_ref.shape
    tokens = x_ref.shape[0]
    if last:
        out_ref[...] = before_ref[...]

    @when_active(step, batches)
    def _(held):
        spare[...] = back_ref[...].astype(F32).reshape(owners * height, lanes)
        rows = gather_rows(spare, owners, height // SLOTS).astype(BF16)
        mixed = lax.dot_general(
            take_ref[held], rows, (((0,), (0,)), ((), ())), preferred_element_type=F32
        )
        result = x_ref[...].astype(F32) + (mixed[:tokens] + mixed[tokens:])
        sent_ref[...] = result.astype(BF16)
        out_ref[held] = result


def onward(step, batches, sections):
    needed = [step - batch for batch in range(batches) if 0 <= step - batch < sections - 1]
    if step % 4 == 1:
        return [(place, place + 1) for place in needed]
    return [(place, (place + 1) % sections) for place in range(sections)]


def body(acts, norm_gain, gate_w, up_w, down_w, route_ids, route_probs):
    sections = lax.axis_size("section")
    owners = lax.axis_size("expert")
    batches, tokens, feature = acts.shape
    picks = route_ids.shape[-1]
    hidden_width = gate_w.shape[-1]
    steps = batches + sections - 1
    height = SLOTS * feature // LANES
    scale = 2.0 / (batches * tokens * picks)
    w_gate, w_up, w_down = gate_w[0, 0], up_w[0, 0], down_w[0, 0]
    packed = jax.ShapeDtypeStruct((owners, height, LANES), BF16)
    held_x = jax.ShapeDtypeStruct((tokens, feature), BF16)
    hidden_shape = jax.ShapeDtypeStruct((batches, SLOTS * owners, hidden_width), BF16)
    layer_shape = jax.ShapeDtypeStruct((batches, tokens, feature), F32)
    spare = [pltpu.VMEM((owners * height, LANES), F32)]

    hiddens = pl.pallas_call(
        weights_kernel,
        out_shape=hidden_shape,
        in_specs=[vmem()] * 3,
        out_specs=vmem(),
        compiler_params=params(2),
        cost_estimate=pl.CostEstimate(
            flops=0, bytes_accessed=4 * 3 * w_gate.size, transcendentals=0
        ),
        name="weights",
    )(w_gate, w_up, w_down)
    send, take, layer_out = pl.pallas_call(
        functools.partial(tables_kernel, owners),
        out_shape=(
            jax.ShapeDtypeStruct((batches, SLOTS * owners, tokens), BF16),
            jax.ShapeDtypeStruct((batches, SLOTS * owners, 2 * tokens), BF16),
            layer_shape,
        ),
        in_specs=[vmem()] * 2,
        out_specs=(vmem(),) * 3,
        compiler_params=params(2),
        name="tables",
    )(jnp.swapaxes(route_ids[0], 1, 2), jnp.swapaxes(route_probs[0], 1, 2))

    sources = [acts]
    for step in range(steps):
        last = step == steps - 1
        outgoing, wide = pl.pallas_call(
            functools.partial(dispatch_kernel, step, owners, batches),
            out_shape=(packed, held_x),
            in_specs=[vmem()] * (len(sources) + 2),
            out_specs=(vmem(), vmem()),
            scratch_shapes=spare,
            compiler_params=params(2),
            name="dispatch",
        )(*sources, norm_gain, send)
        incoming = lax.all_to_all(outgoing, "expert", split_axis=0, concat_axis=0, tiled=True)
        output, hiddens = pl.pallas_call(
            functools.partial(expert_kernel, step, batches),
            out_shape=(packed, hidden_shape),
            in_specs=[vmem()] * 5,
            out_specs=(vmem(), vmem()),
            scratch_shapes=spare,
            input_output_aliases={4: 1},
            compiler_params=params(2),
            name="expert",
        )(incoming, w_gate, w_up, w_down, hiddens)
        back = lax.all_to_all(output, "expert", split_axis=0, concat_axis=0, tiled=True)
        sent, layer_out = pl.pallas_call(
            functools.partial(combine_kernel, step, batches, last),
            out_shape=(held_x, layer_shape),
            in_specs=[vmem()] * 4,
            out_specs=(vmem(), vmem()),
            scratch_shapes=spare,
            input_output_aliases={} if last else {3: 1},
            compiler_params=params(2),
            name="combine",
        )(wide, back, take, layer_out)
        if not last:
            arrived = lax.ppermute(sent, "section", onward(step, batches, sections))
            sources = [arrived, acts] if step + 1 < batches else [arrived]
    rows = hiddens.reshape(batches * SLOTS * owners, hidden_width)
    square = lax.dot_general(rows, rows, (((0,), (0,)), ((), ())), preferred_element_type=F32)
    return (layer_out[None], (scale * square)[None, None])


def solution(mesh):
    placed = (
        P(None, "expert", None),
        P("section", None),
        P("section", "expert", None, None),
        P("section", "expert", None, None),
        P("section", "expert", None, None),
        P("section", None, "expert", None),
        P("section", None, "expert", None),
    )
    return jax.shard_map(
        body,
        mesh=mesh,
        in_specs=placed,
        out_specs=(P("section", None, "expert", None), P("section", "expert", None, None)),
        check_vma=False,
    )
```

```python
import functools

import jax
import jax.numpy as jnp
from jax import lax
from jax.experimental import pallas as pl
from jax.experimental.pallas import tpu as pltpu
from jax.sharding import PartitionSpec as P

LANES = 128
SLOTS = 2
BF16 = jnp.bfloat16
F32 = jnp.float32


MIB = 1 << 20


def params(mib):
    return pltpu.CompilerParams(vmem_limit_bytes=mib * MIB)


def vmem():
    return pl.BlockSpec(memory_space=pltpu.VMEM)


def spread_rows(rows, spare, owners):
    blocks = rows.shape[1] // LANES
    for slot in range(SLOTS):
        for block in range(blocks):
            spare[pl.ds(slot * blocks + block, owners, stride=SLOTS * blocks), :] = rows[
                slot * owners : (slot + 1) * owners, block * LANES : (block + 1) * LANES
            ]


def gather_rows(spare, owners, blocks):
    parts = []
    for slot in range(SLOTS):
        parts.append(
            jnp.concatenate(
                [
                    spare[pl.ds(slot * blocks + block, owners, stride=SLOTS * blocks), :]
                    for block in range(blocks)
                ],
                axis=1,
            )
        )
    return jnp.concatenate(parts, axis=0)


def stay(value):
    return pltpu.with_memory_space_constraint(value, pltpu.HBM)


def copies(sources, targets, sems):
    return [
        pltpu.make_async_copy(source, target, sems.at[place])
        for place, (source, target) in enumerate(zip(sources, targets))
    ]


def slot_tables(owners, ids, probs):
    picks, tokens = ids.shape
    experts = lax.broadcasted_iota(jnp.int32, (owners, tokens), 0)
    earlier = (
        lax.broadcasted_iota(jnp.int32, (tokens, tokens), 0)
        < lax.broadcasted_iota(jnp.int32, (tokens, tokens), 1)
    ).astype(BF16)
    named = jnp.zeros((owners, tokens), F32)
    weight = jnp.zeros((owners, tokens), F32)
    for pick in range(picks):
        hit = ids[pick : pick + 1, :] == experts
        named = named + jnp.where(hit, 1.0, 0.0)
        weight = weight + jnp.where(hit, probs[pick : pick + 1, :], 0.0)
    slot = jnp.dot(named.astype(BF16), earlier, preferred_element_type=F32)
    split = [jnp.abs(slot - number) < 0.5 for number in range(SLOTS)]
    send = jnp.concatenate([jnp.where(own, named, 0.0) for own in split], axis=0)
    take = jnp.concatenate([jnp.where(own, weight, 0.0) for own in split], axis=0)
    high = take.astype(BF16).astype(F32)
    return send.astype(BF16), jnp.concatenate([high, take - high], axis=1).astype(BF16)


def dispatch_rows(x, gain, send, out_ref, spare):
    wide = x.astype(F32)
    mean = jnp.mean(wide * wide, axis=-1, keepdims=True)
    normed = (wide * lax.rsqrt(mean + 1e-06) * gain).astype(BF16)
    rows = jnp.dot(send, normed, preferred_element_type=F32)
    spread_rows(rows, spare, out_ref.shape[0])
    out_ref[...] = spare[...].astype(BF16).reshape(out_ref.shape)


def first_kernel(
    ids_hbm,
    probs_hbm,
    acts_hbm,
    gain_hbm,
    _gate,
    _up,
    _down,
    out_ref,
    acts_ref,
    gain_ref,
    send_ref,
    take_ref,
    hidden_ref,
    layer_ref,
    ids_ref,
    probs_ref,
    spare,
    sems,
):
    moves = copies(
        (ids_hbm, probs_hbm, acts_hbm, gain_hbm), (ids_ref, probs_ref, acts_ref, gain_ref), sems
    )
    for move in moves:
        move.start()
    for ref in (hidden_ref, layer_ref):
        ref[...] = jnp.zeros_like(ref)
    for move in moves:
        move.wait()
    for batch in range(ids_ref.shape[0]):
        send_ref[batch], take_ref[batch] = slot_tables(
            out_ref.shape[0], ids_ref[batch], probs_ref[batch]
        )
    dispatch_rows(acts_ref[0], gain_ref[...], send_ref[0], out_ref, spare)


def when_active(step, batches):
    batch = step - lax.axis_index("section")

    def call(function):
        pl.when((batch >= 0) & (batch < batches))(lambda: function(batch))

    return call


def dispatch_kernel(step, batches, *refs):
    arrived_ref, *acts, gain_ref, send_ref, out_ref, x_ref, spare = refs

    @when_active(step, batches)
    def _(held):
        x = arrived_ref[...]
        if acts:
            x = jnp.where(held == step, acts[0][step], x)
        x_ref[...] = x
        dispatch_rows(x, gain_ref[...], send_ref[held], out_ref, spare)


def expert_kernel(step, batches, in_ref, gate_ref, up_ref, down_ref, _, out_ref, hidden_ref, spare):
    owners, height, lanes = in_ref.shape

    @when_active(step, batches)
    def _(held):
        spare[...] = in_ref[...].astype(F32).reshape(owners * height, lanes)
        rows = gather_rows(spare, owners, height // SLOTS).astype(BF16)
        gate = jnp.dot(rows, gate_ref[...], preferred_element_type=F32)
        upper = jnp.dot(rows, up_ref[...], preferred_element_type=F32)
        hidden = (gate / (1.0 + jnp.exp(-gate)) * upper).astype(BF16)
        hidden_ref[held] = hidden
        output = jnp.dot(hidden, down_ref[...], preferred_element_type=F32)
        spread_rows(output, spare, owners)
        out_ref[...] = spare[...].astype(BF16).reshape(out_ref.shape)


def combine_kernel(
    step, batches, last, x_ref, back_ref, take_ref, before_ref, sent_ref, out_ref, spare
):
    owners, height, lanes = back_ref.shape
    tokens = x_ref.shape[-2]
    if last:
        out_ref[...] = before_ref[...]

    @when_active(step, batches)
    def _(held):
        spare[...] = back_ref[...].astype(F32).reshape(owners * height, lanes)
        rows = gather_rows(spare, owners, height // SLOTS).astype(BF16)
        mixed = lax.dot_general(
            take_ref[held], rows, (((0,), (0,)), ((), ())), preferred_element_type=F32
        )
        x = x_ref[...] if step > 0 else x_ref[0]
        result = x.astype(F32) + (mixed[:tokens] + mixed[tokens:])
        sent_ref[...] = result.astype(BF16)
        out_ref[held] = result


def onward(step, batches, sections):
    needed = [step - batch for batch in range(batches) if 0 <= step - batch < sections - 1]
    if step % 4 == 1:
        return [(place, place + 1) for place in needed]
    return [(place, (place + 1) % sections) for place in range(sections)]


def body(acts, norm_gain, gate_w, up_w, down_w, route_ids, route_probs):
    sections = lax.axis_size("section")
    owners = lax.axis_size("expert")
    batches, tokens, feature = acts.shape
    picks = route_ids.shape[-1]
    hidden_width = gate_w.shape[-1]
    steps = batches + sections - 1
    height = SLOTS * feature // LANES
    scale = 2.0 / (batches * tokens * picks)
    weights = (gate_w[0, 0], up_w[0, 0], down_w[0, 0])
    packed = jax.ShapeDtypeStruct((owners, height, LANES), BF16)
    held_x = jax.ShapeDtypeStruct((tokens, feature), BF16)
    hidden_shape = jax.ShapeDtypeStruct((batches, SLOTS * owners, hidden_width), BF16)
    layer_shape = jax.ShapeDtypeStruct((batches, tokens, feature), F32)
    spare = [pltpu.VMEM((owners * height, LANES), F32)]

    hbm = pl.BlockSpec(memory_space=pltpu.HBM)
    ids = jnp.swapaxes(route_ids[0], 1, 2)
    probs = jnp.swapaxes(route_probs[0], 1, 2)
    outgoing, local_acts, gain, send, take, hiddens, layer_out = pl.pallas_call(
        first_kernel,
        out_shape=(
            packed,
            jax.ShapeDtypeStruct(acts.shape, acts.dtype),
            jax.ShapeDtypeStruct(norm_gain.shape, norm_gain.dtype),
            jax.ShapeDtypeStruct((batches, SLOTS * owners, tokens), BF16),
            jax.ShapeDtypeStruct((batches, SLOTS * owners, 2 * tokens), BF16),
            hidden_shape,
            layer_shape,
        ),
        in_specs=[hbm] * 7,
        out_specs=(vmem(),) * 7,
        scratch_shapes=[
            pltpu.VMEM(ids.shape, ids.dtype),
            pltpu.VMEM(probs.shape, probs.dtype),
            *spare,
            pltpu.SemaphoreType.DMA((4,)),
        ],
        compiler_params=params(2),
        name="first",
    )(*map(stay, (ids, probs, acts, norm_gain, *weights)))
    wide = local_acts

    for step in range(steps):
        last = step == steps - 1
        if step > 0:
            sources = [arrived, local_acts] if step < batches else [arrived]
            outgoing, wide = pl.pallas_call(
                functools.partial(dispatch_kernel, step, batches),
                out_shape=(packed, held_x),
                in_specs=[vmem()] * (len(sources) + 2),
                out_specs=(vmem(), vmem()),
                scratch_shapes=spare,
                compiler_params=params(2),
                name="dispatch",
            )(*sources, gain, send)
        incoming = lax.all_to_all(outgoing, "expert", split_axis=0, concat_axis=0, tiled=True)
        output, hiddens = pl.pallas_call(
            functools.partial(expert_kernel, step, batches),
            out_shape=(packed, hidden_shape),
            in_specs=[vmem()] * 5,
            out_specs=(vmem(), vmem()),
            scratch_shapes=spare,
            input_output_aliases={4: 1},
            compiler_params=params(2),
            name="expert",
        )(incoming, *weights, hiddens)
        back = lax.all_to_all(output, "expert", split_axis=0, concat_axis=0, tiled=True)
        sent, layer_out = pl.pallas_call(
            functools.partial(combine_kernel, step, batches, last),
            out_shape=(held_x, layer_shape),
            in_specs=[vmem()] * 4,
            out_specs=(vmem(), vmem()),
            scratch_shapes=spare,
            input_output_aliases={} if last else {3: 1},
            compiler_params=params(2),
            name="combine",
        )(wide, back, take, layer_out)
        if not last:
            arrived = lax.ppermute(sent, "section", onward(step, batches, sections))
    rows = hiddens.reshape(batches * SLOTS * owners, hidden_width)
    square = lax.dot_general(rows, rows, (((0,), (0,)), ((), ())), preferred_element_type=F32)
    return (layer_out[None], (scale * square)[None, None])


def solution(mesh):
    placed = (
        P(None, "expert", None),
        P("section", None),
        P("section", "expert", None, None),
        P("section", "expert", None, None),
        P("section", "expert", None, None),
        P("section", None, "expert", None),
        P("section", None, "expert", None),
    )
    return jax.shard_map(
        body,
        mesh=mesh,
        in_specs=placed,
        out_specs=(P("section", None, "expert", None), P("section", "expert", None, None)),
        check_vma=False,
    )
```

```python
import functools

import jax
import jax.numpy as jnp
from jax import lax
from jax.experimental import pallas as pl
from jax.experimental.pallas import tpu as pltpu
from jax.sharding import PartitionSpec as P

LANES = 128
SLOTS = 2
BF16 = jnp.bfloat16
F32 = jnp.float32


MIB = 1 << 20


def params(mib):
    return pltpu.CompilerParams(vmem_limit_bytes=mib * MIB)


def vmem():
    return pl.BlockSpec(memory_space=pltpu.VMEM)


def spread_rows(rows, spare, owners):
    blocks = rows.shape[1] // LANES
    for slot in range(SLOTS):
        for block in range(blocks):
            spare[pl.ds(slot * blocks + block, owners, stride=SLOTS * blocks), :] = rows[
                slot * owners : (slot + 1) * owners, block * LANES : (block + 1) * LANES
            ]


def gather_rows(spare, owners, blocks):
    parts = []
    for slot in range(SLOTS):
        parts.append(
            jnp.concatenate(
                [
                    spare[pl.ds(slot * blocks + block, owners, stride=SLOTS * blocks), :]
                    for block in range(blocks)
                ],
                axis=1,
            )
        )
    return jnp.concatenate(parts, axis=0)


def stay(value):
    return pltpu.with_memory_space_constraint(value, pltpu.HBM)


def copies(sources, targets, sems):
    return [
        pltpu.make_async_copy(source, target, sems.at[place])
        for place, (source, target) in enumerate(zip(sources, targets))
    ]


def slot_tables(owners, ids, probs):
    picks, tokens = ids.shape
    experts = lax.broadcasted_iota(jnp.int32, (owners, tokens), 0)
    earlier = (
        lax.broadcasted_iota(jnp.int32, (tokens, tokens), 0)
        < lax.broadcasted_iota(jnp.int32, (tokens, tokens), 1)
    ).astype(BF16)
    named = jnp.zeros((owners, tokens), F32)
    weight = jnp.zeros((owners, tokens), F32)
    for pick in range(picks):
        hit = ids[pick : pick + 1, :] == experts
        named = named + jnp.where(hit, 1.0, 0.0)
        weight = weight + jnp.where(hit, probs[pick : pick + 1, :], 0.0)
    slot = jnp.dot(named.astype(BF16), earlier, preferred_element_type=F32)
    split = [jnp.abs(slot - number) < 0.5 for number in range(SLOTS)]
    send = jnp.concatenate([jnp.where(own, named, 0.0) for own in split], axis=0)
    take = jnp.concatenate([jnp.where(own, weight, 0.0) for own in split], axis=0)
    high = take.astype(BF16).astype(F32)
    return send.astype(BF16), jnp.concatenate([high, take - high], axis=1).astype(BF16)


def dispatch_rows(x, gain, send, out_ref, spare):
    wide = x.astype(F32)
    mean = jnp.mean(wide * wide, axis=-1, keepdims=True)
    normed = (wide * lax.rsqrt(mean + 1e-06) * gain).astype(BF16)
    rows = jnp.dot(send, normed, preferred_element_type=F32)
    spread_rows(rows, spare, out_ref.shape[0])
    out_ref[...] = spare[...].astype(BF16).reshape(out_ref.shape)


def first_kernel(
    ids_hbm,
    probs_hbm,
    acts_hbm,
    gain_hbm,
    _gate,
    _up,
    _down,
    out_ref,
    acts_ref,
    gain_ref,
    send_ref,
    take_ref,
    hidden_ref,
    layer_ref,
    ids_ref,
    probs_ref,
    spare,
    sems,
):
    moves = copies(
        (ids_hbm, probs_hbm, acts_hbm, gain_hbm), (ids_ref, probs_ref, acts_ref, gain_ref), sems
    )
    for move in moves:
        move.start()
    for ref in (hidden_ref, layer_ref):
        ref[...] = jnp.zeros_like(ref)
    for move in moves:
        move.wait()
    for batch in range(ids_ref.shape[0]):
        send_ref[batch], take_ref[batch] = slot_tables(
            out_ref.shape[0], ids_ref[batch], probs_ref[batch]
        )
    dispatch_rows(acts_ref[0], gain_ref[...], send_ref[0], out_ref, spare)


def when_active(step, batches):
    batch = step - lax.axis_index("section")

    def call(function):
        pl.when((batch >= 0) & (batch < batches))(lambda: function(batch))

    return call


def dispatch_kernel(step, batches, *refs):
    arrived_ref, *acts, gain_ref, send_ref, out_ref, x_ref, spare = refs

    @when_active(step, batches)
    def _(held):
        x = arrived_ref[...]
        if acts:
            x = jnp.where(held == step, acts[0][step], x)
        x_ref[...] = x
        dispatch_rows(x, gain_ref[...], send_ref[held], out_ref, spare)


def expert_kernel(step, batches, in_ref, gate_ref, up_ref, down_ref, _, out_ref, hidden_ref, spare):
    owners, height, lanes = in_ref.shape

    @when_active(step, batches)
    def _(held):
        spare[...] = in_ref[...].astype(F32).reshape(owners * height, lanes)
        rows = gather_rows(spare, owners, height // SLOTS).astype(BF16)
        gate = jnp.dot(rows, gate_ref[...], preferred_element_type=F32)
        upper = jnp.dot(rows, up_ref[...], preferred_element_type=F32)
        hidden = (gate / (1.0 + jnp.exp(-gate)) * upper).astype(BF16)
        hidden_ref[held] = hidden
        output = jnp.dot(hidden, down_ref[...], preferred_element_type=F32)
        spread_rows(output, spare, owners)
        out_ref[...] = spare[...].astype(BF16).reshape(out_ref.shape)


def combine_kernel(
    step, batches, last, x_ref, back_ref, take_ref, before_ref, sent_ref, out_ref, spare
):
    owners, height, lanes = back_ref.shape
    tokens = x_ref.shape[-2]
    if last:
        out_ref[...] = before_ref[...]

    @when_active(step, batches)
    def _(held):
        spare[...] = back_ref[...].astype(F32).reshape(owners * height, lanes)
        rows = gather_rows(spare, owners, height // SLOTS).astype(BF16)
        mixed = lax.dot_general(
            take_ref[held], rows, (((0,), (0,)), ((), ())), preferred_element_type=F32
        )
        x = x_ref[...] if step > 0 else x_ref[0]
        result = x.astype(F32) + (mixed[:tokens] + mixed[tokens:])
        sent_ref[...] = result.astype(BF16)
        out_ref[held] = result


def onward(step, batches, sections):
    needed = [step - batch for batch in range(batches) if 0 <= step - batch < sections - 1]
    if step in (1, 5):
        return [(place, place + 1) for place in needed]
    return [(place, (place + 1) % sections) for place in range(sections)]


def groups_of(step, batches, sections, owners):
    row = 4 if sections % 4 == 0 and owners % 4 == 0 else 1
    lots = owners // row
    working = {(step - batch) // row for batch in range(batches)}
    groups = []
    for first in range(0, sections, row):
        places = range(first, first + row)
        if first // row in working:
            groups += [[place * owners + own for own in range(owners)] for place in places]
        else:
            groups += [
                [place * owners + lot * lots + own for place in places for own in range(lots)]
                for lot in range(row)
            ]
    return groups


def body(acts, norm_gain, gate_w, up_w, down_w, route_ids, route_probs):
    sections = lax.axis_size("section")
    owners = lax.axis_size("expert")
    batches, tokens, feature = acts.shape
    picks = route_ids.shape[-1]
    hidden_width = gate_w.shape[-1]
    steps = batches + sections - 1
    height = SLOTS * feature // LANES
    scale = 2.0 / (batches * tokens * picks)
    weights = (gate_w[0, 0], up_w[0, 0], down_w[0, 0])
    packed = jax.ShapeDtypeStruct((owners, height, LANES), BF16)
    held_x = jax.ShapeDtypeStruct((tokens, feature), BF16)
    hidden_shape = jax.ShapeDtypeStruct((batches, SLOTS * owners, hidden_width), BF16)
    layer_shape = jax.ShapeDtypeStruct((batches, tokens, feature), F32)
    spare = [pltpu.VMEM((owners * height, LANES), F32)]

    hbm = pl.BlockSpec(memory_space=pltpu.HBM)
    ids = jnp.swapaxes(route_ids[0], 1, 2)
    probs = jnp.swapaxes(route_probs[0], 1, 2)
    outgoing, local_acts, gain, send, take, hiddens, layer_out = pl.pallas_call(
        first_kernel,
        out_shape=(
            packed,
            jax.ShapeDtypeStruct(acts.shape, acts.dtype),
            jax.ShapeDtypeStruct(norm_gain.shape, norm_gain.dtype),
            jax.ShapeDtypeStruct((batches, SLOTS * owners, tokens), BF16),
            jax.ShapeDtypeStruct((batches, SLOTS * owners, 2 * tokens), BF16),
            hidden_shape,
            layer_shape,
        ),
        in_specs=[hbm] * 7,
        out_specs=(vmem(),) * 7,
        scratch_shapes=[
            pltpu.VMEM(ids.shape, ids.dtype),
            pltpu.VMEM(probs.shape, probs.dtype),
            *spare,
            pltpu.SemaphoreType.DMA((4,)),
        ],
        compiler_params=params(2),
        name="first",
    )(*map(stay, (ids, probs, acts, norm_gain, *weights)))
    wide = local_acts

    for step in range(steps):
        last = step == steps - 1
        if step > 0:
            sources = [arrived, local_acts] if step < batches else [arrived]
            outgoing, wide = pl.pallas_call(
                functools.partial(dispatch_kernel, step, batches),
                out_shape=(packed, held_x),
                in_specs=[vmem()] * (len(sources) + 2),
                out_specs=(vmem(), vmem()),
                scratch_shapes=spare,
                compiler_params=params(2),
                name="dispatch",
            )(*sources, gain, send)
        incoming = lax.all_to_all(
            outgoing, ("section", "expert"), split_axis=0, concat_axis=0, tiled=True,
            axis_index_groups=groups_of(step, batches, sections, owners),
        )
        output, hiddens = pl.pallas_call(
            functools.partial(expert_kernel, step, batches),
            out_shape=(packed, hidden_shape),
            in_specs=[vmem()] * 5,
            out_specs=(vmem(), vmem()),
            scratch_shapes=spare,
            input_output_aliases={4: 1},
            compiler_params=params(2),
            name="expert",
        )(incoming, *weights, hiddens)
        back = lax.all_to_all(
            output, ("section", "expert"), split_axis=0, concat_axis=0, tiled=True,
            axis_index_groups=groups_of(step, batches, sections, owners),
        )
        sent, layer_out = pl.pallas_call(
            functools.partial(combine_kernel, step, batches, last),
            out_shape=(held_x, layer_shape),
            in_specs=[vmem()] * 4,
            out_specs=(vmem(), vmem()),
            scratch_shapes=spare,
            input_output_aliases={} if last else {3: 1},
            compiler_params=params(2),
            name="combine",
        )(wide, back, take, layer_out)
        if not last:
            arrived = lax.ppermute(sent, "section", onward(step, batches, sections))
    rows = hiddens.reshape(batches * SLOTS * owners, hidden_width)
    square = lax.dot_general(rows, rows, (((0,), (0,)), ((), ())), preferred_element_type=F32)
    return (layer_out[None], (scale * square)[None, None])


def solution(mesh):
    placed = (
        P(None, "expert", None),
        P("section", None),
        P("section", "expert", None, None),
        P("section", "expert", None, None),
        P("section", "expert", None, None),
        P("section", None, "expert", None),
        P("section", None, "expert", None),
    )
    return jax.shard_map(
        body,
        mesh=mesh,
        in_specs=placed,
        out_specs=(P("section", None, "expert", None), P("section", "expert", None, None)),
        check_vma=False,
    )
```
